512 devices in a mesh: ctx: 64 (over x, z), dp: 8 (over y, core).
Axes of the slice: x: 4, y: 4, z: 16, core: 2. Of those that a mesh axis runs over, the one named last changes fastest.
Arguments:
- queries: bfloat16 [24576, 8192], P(('ctx', 'dp')), may hold values from -8 to 8
- keys: bfloat16 [24576, 1024], P('ctx', 'dp'), may hold values from -4 to 4
- values: bfloat16 [24576, 1024], P('ctx', 'dp'), may hold values from -6 to 6
- block_list: int32 [192, 13], P('ctx'), may hold values from 0 to 191, as said below
Outputs:
- attended: bfloat16 [24576, 8192], P(('ctx', 'dp'))
The draws below stay inside these ranges and needn't reach their ends.
Inputs may be any that keep to these rules, and one draw needn't show every extreme that they name: `block_list`: entries 0 to 2 of row n are n - 1, n and n + 1 modulo 192; entries 3 and 4 are 0 and 1; entries 5 to 12 are random blocks. The random blocks listed by the 3 query blocks of one context shard lie in other shards, at most 1 of them in any one shard, and exactly 1 in some shard.
All inputs are finite; a program needn't handle non-finite values.
Results may differ from the reference program's by a relative error of at most 0.0049.
Values may be sent and summed in bfloat16 or wider, within the bound.
A program may use at most 128 MiB of HBM per device.

```python
import math
import jax
import jax.numpy as jnp
from jax import lax

HEADS = 64
KV_HEADS = 8
HEAD_DIM = 128
BLOCK = 128
RAND = 8
KB_DEV = 3
LIST = 13
BLOCKS = 192
SEQ = 24576


def draw_keys(key, part):
    base = jnp.clip(jax.random.normal(jax.random.fold_in(key, 11), (SEQ, KV_HEADS, HEAD_DIM), jnp.float32), -4.0, 4.0)
    return base.reshape(SEQ, KV_HEADS * HEAD_DIM).astype(jnp.bfloat16)


def draw_queries(key, part):
    group_size = HEADS // KV_HEADS
    base = jnp.clip(jax.random.normal(jax.random.fold_in(key, 12), (SEQ, KV_HEADS, group_size, HEAD_DIM), jnp.float32), -4.0, 4.0)
    return base.reshape(SEQ, HEADS * HEAD_DIM).astype(jnp.bfloat16)


def draw_block_list(key, part):
    shards = BLOCKS // KB_DEV
    request_count = KB_DEV * RAND
    rows = jnp.arange(BLOCKS, dtype=jnp.int32)
    window_ids = jnp.stack([(rows - 1) % BLOCKS, rows, (rows + 1) % BLOCKS], axis=1)
    global_ids = jnp.zeros((BLOCKS, 2), jnp.int32) + jnp.array([0, 1], jnp.int32)[None, :]
    hot_order = jax.random.permutation(jax.random.fold_in(key, 21), shards)
    hot_flags = (hot_order < max(1, shards // 8)).astype(jnp.int32)
    step_ids = jnp.arange(shards - 1, dtype=jnp.int32)
    requesters = jnp.arange(shards, dtype=jnp.int32)
    owners = (requesters[:, None] + 1 + step_ids[None, :]) % shards
    scores = jax.random.randint(jax.random.fold_in(key, 22), (shards, shards - 1), 0, 1 << 20, dtype=jnp.int32)
    scores = scores + hot_flags[owners] * (1 << 20)
    scores = scores * shards + step_ids[None, :]
    ordering = jnp.argsort(-scores, axis=1)
    ranked = jnp.take_along_axis(owners, ordering, axis=1)
    picks = jnp.arange(request_count) % (shards - 1)
    chosen = ranked[:, picks]
    offsets = jax.random.randint(jax.random.fold_in(key, 23), (shards, request_count), 0, KB_DEV, dtype=jnp.int32)
    random_ids = (chosen * KB_DEV + offsets).reshape(BLOCKS, RAND)
    return jnp.concatenate([window_ids, global_ids, random_ids], axis=1).astype(jnp.int32)


def block_levels(stream_key, extent, split, low, top_value):
    def one(axis_at, shards_of):
        steps = jax.random.uniform(jax.random.fold_in(jax.random.fold_in(stream_key, 6), axis_at), (shards_of,), jnp.float32, low / len(split), top_value / len(split))
        return jnp.repeat(jnp.exp(steps), extent[axis_at] // shards_of).reshape((-1,) + (1,) * (len(extent) - axis_at - 1))

    gain = one(*split[0])
    for cut in split[1:]:
        gain = gain * one(*cut)
    return gain


def scatter_about(key, shape, width, bound, cuts=(), kind=jnp.bfloat16):
    level = block_levels(key, shape, cuts, -0.22, 0.18) if cuts else 1.0
    entries = jax.random.normal(key, shape, jnp.float32) * width * level
    return jnp.minimum(jnp.maximum(entries, -bound), bound).astype(kind)


def setup_inputs(seed: int = 0) -> dict:
    seeds = jax.random.split(jax.random.key(seed), 5)
    return {
        "queries": draw_queries(jax.random.fold_in(seeds[4], 71), 0),
        "keys": draw_keys(jax.random.fold_in(seeds[4], 71), 0),
        "values": scatter_about(seeds[2], (SEQ, KV_HEADS * HEAD_DIM), 1.0, 6.0, ((0, 64), (1, 8))),
        "block_list": draw_block_list(jax.random.fold_in(seeds[4], 71), 0),
    }


def reference(queries, keys, values, block_list):
    group_size = HEADS // KV_HEADS
    score_scale = 1.0 / math.sqrt(HEAD_DIM)
    key_blocks = keys.reshape(BLOCKS, BLOCK, KV_HEADS, HEAD_DIM)
    value_blocks = values.reshape(BLOCKS, BLOCK, KV_HEADS, HEAD_DIM)
    query_blocks = queries.reshape(BLOCKS, BLOCK, KV_HEADS, group_size, HEAD_DIM)
    earlier = jnp.arange(LIST)[:, None] > jnp.arange(LIST)[None, :]

    def one_block(inputs):
        q_block, block_ids = inputs
        repeats = (block_ids[:, None] == block_ids[None, :]) & earlier
        keep_block = jnp.logical_not(jnp.any(repeats, axis=1))
        key_mask = jnp.repeat(keep_block, BLOCK)
        key_rows = key_blocks[block_ids].reshape(LIST * BLOCK, KV_HEADS, HEAD_DIM)
        value_rows = value_blocks[block_ids].reshape(LIST * BLOCK, KV_HEADS, HEAD_DIM)
        scores = jnp.einsum('tkgd,skd->kgts', q_block.astype(jnp.float32), key_rows.astype(jnp.float32)) * score_scale
        row_max = lax.optimization_barrier(jnp.max(jnp.where(key_mask, scores, -jnp.inf), axis=-1, keepdims=True))
        unnormed = jnp.where(key_mask, jnp.exp(scores - row_max), 0.0)
        row_sum = lax.optimization_barrier(jnp.sum(unnormed, axis=-1, keepdims=True))
        weights = (unnormed / row_sum).astype(jnp.bfloat16)
        result = jnp.einsum('kgts,skd->tkgd', weights.astype(jnp.float32), value_rows.astype(jnp.float32))
        return result.astype(jnp.bfloat16).reshape(BLOCK, HEADS * HEAD_DIM)
    attended = lax.map(one_block, (query_blocks, block_list))
    return attended.reshape(SEQ, HEADS * HEAD_DIM)
```

```python
import math

import jax
import jax.numpy as jnp
from jax import lax
from jax.experimental import pallas as pl
from jax.experimental.pallas import tpu as pltpu
from jax.sharding import PartitionSpec as P

HEAD_DIM = 128
BLOCK = 128
LIST = 13
KB = 3
GROUP = 8
NX, NZ, NDP = 4, 16, 8
TOK = 48
WIDTH = GROUP * HEAD_DIM
SPAN = KB * BLOCK
OWN = NZ * KB
RECV = OWN
GLOB = RECV + NX * NZ
EDGE = GLOB + 2
SLOTS = EDGE + 1
PAIR = 2
STEPS = GROUP // PAIR
MESH = pl.DeviceIdType.MESH


def kernel(list_ref, q_ref, k_ref, v_ref, out_ref, kv, picked, kcat, vcat, qbuf, obuf, ask, asked, asked_s,
           load_sem, own_q_sem, own_out_sem, ask_send, ask_recv, asked_sem, q_send, q_recv, z_send, z_half_send, z_recv,
           z_half_recv, x_send, x_recv, glob_send, glob_recv, edge_send, edge_recv, out_send, out_recv):
    c = lax.axis_index("ctx")
    p = lax.axis_index("dp")
    x = c // NZ
    z = c % NZ

    def at_x(d):
        return {"ctx": lax.rem(x + d, NX) * NZ + z, "dp": p}

    def at_z(d):
        return {"ctx": x * NZ + lax.rem(z + d, NZ), "dp": p}

    def at_p(d):
        return {"ctx": c, "dp": lax.rem(p + d, NDP)}

    def send(src, dst, ssem, rsem, dev):
        return pltpu.make_async_remote_copy(
            src_ref=src, dst_ref=dst, send_sem=ssem, recv_sem=rsem, device_id=dev, device_id_type=MESH
        )

    barrier = pltpu.get_barrier_semaphore()
    for d in range(1, NX):
        pl.semaphore_signal(barrier, inc=1, device_id=at_x(d), device_id_type=MESH)
    for d in (1, NZ - 1):
        pl.semaphore_signal(barrier, inc=1, device_id=at_z(d), device_id_type=MESH)
    for d in range(1, NDP):
        pl.semaphore_signal(barrier, inc=1, device_id=at_p(d), device_id_type=MESH)

    loads = []
    for b in range(KB):
        slot = z * KB + b
        loads.append(pltpu.make_async_copy(k_ref.at[b], kv.at[slot, pl.ds(0, BLOCK)], load_sem.at[0, b]))
        loads.append(pltpu.make_async_copy(v_ref.at[b], kv.at[slot, pl.ds(BLOCK, BLOCK)], load_sem.at[1, b]))
    for copy in loads:
        copy.start()
    own_q = pltpu.make_async_copy(
        q_ref.at[:, pl.ds(pl.multiple_of(p * WIDTH, WIDTH), WIDTH)],
        qbuf.at[pl.ds(pl.multiple_of(p * TOK, 16), TOK)], own_q_sem)
    own_q.start()

    rows = lax.broadcasted_iota(jnp.int32, (NX * NZ, 128), 0) * KB
    wanted = jnp.zeros((NX * NZ, 128), jnp.int32)
    for i in range(KB):
        for e in range(5, LIST):
            off = list_ref[i, e] - rows
            wanted = wanted + jnp.where(off == 1, 1, 0) + jnp.where(off == 2, 2, 0)
    ask[...] = wanted.reshape(NX, NZ, 128)

    for copy in loads:
        copy.wait()
    pl.semaphore_wait(barrier, NX - 1 + 2 + NDP - 1)

    asks = []
    for d in range(1, NX):
        asks.append(send(ask.at[lax.rem(x + d, NX)], asked.at[d], ask_send.at[d], ask_recv.at[d], at_x(d)))
        asks[-1].start()

    def z_block(slot, up, k, b):
        way = 0 if up else 1
        s = slot * KB + b
        return send(kv.at[s], kv.at[s], z_send.at[way], z_recv.at[way, k, b], at_z(1 if up else NZ - 1))

    def z_half(slot, up, b):
        way = 0 if up else 1
        s = slot * KB + b
        part = pl.ds(0 if up else BLOCK, BLOCK)
        return send(kv.at[s, part], kv.at[s, part], z_half_send.at[way], z_half_recv.at[way, b],
                    at_z(1 if up else NZ - 1))

    for b in range(KB):
        for up in (True, False):
            z_block(z, up, 1, b).start()

    q_copies = []
    for d in range(1, NDP):
        t = lax.rem(p + d, NDP)
        q_copies.append(send(
            q_ref.at[:, pl.ds(pl.multiple_of(t * WIDTH, WIDTH), WIDTH)],
            qbuf.at[pl.ds(pl.multiple_of(p * TOK, 16), TOK)],
            q_send.at[d], q_recv.at[d], at_p(d)))
        q_copies[-1].start()

    for copy in asks:
        copy.wait()
    to_scalars = pltpu.make_async_copy(asked, asked_s, asked_sem)
    to_scalars.start()
    to_scalars.wait()

    def glob_copy(d):
        return send(kv.at[pl.ds(0, 2)], kv.at[pl.ds(GLOB, 2)], glob_send.at[d], glob_recv, at_x(d))

    def edge_copy(slot, d):
        return send(kv.at[slot], kv.at[EDGE], edge_send, edge_recv, at_x(d))

    def share(slot):
        first, second, third = (kv[slot * KB + b] for b in range(KB))
        for d in (2, 1, 3):
            off = asked_s[NX - d, slot, 0]
            picked[d - 1, slot] = jnp.where(off == 1, second, jnp.where(off == 2, third, first))
            send(picked.at[d - 1, slot], kv.at[RECV + x * NZ + slot], x_send.at[d - 1], x_recv.at[d - 1],
                 at_x(d)).start()

        @pl.when((x == 0) & (slot == 0))
        def _():
            for d in range(1, NX):
                glob_copy(d).start()

        @pl.when((z == 0) & (slot == NZ - 1))
        def _():
            edge_copy((NZ - 1) * KB + KB - 1, 1).start()

        @pl.when((z == NZ - 1) & (slot == 0))
        def _():
            edge_copy(0, NX - 1).start()

    share(z)

    @pl.loop(1, NZ // 2)
    def _(k):
        above = lax.rem(z + NZ - k, NZ)
        below = lax.rem(z + k, NZ)
        for b in range(KB):
            for up, slot in ((True, above), (False, below)):
                z_block(slot, up, k, b).wait_recv()

                @pl.when(k < NZ // 2 - 1)
                def _():
                    z_block(slot, up, k + 1, b).start()

                @pl.when(k == NZ // 2 - 1)
                def _():
                    z_half(slot, up, b).start()

        share(above)
        share(below)

    far = lax.rem(z + NZ // 2, NZ)
    for b in range(KB):
        for up in (True, False):
            z_half(far, up, b).wait_recv()
    share(far)

    for copy in q_copies:
        copy.wait()
    own_q.wait()

    for d in range(1, NX):
        source = lax.rem(x + NX - d, NX)
        landed = kv.at[pl.ds(RECV + source * NZ, NZ)]
        send(picked.at[d - 1], landed, x_send.at[d - 1], x_recv.at[d - 1], at_x(d)).wait()

    @pl.when(x != 0)
    def _():
        glob_copy(1).wait_recv()

    @pl.when((z == 0) | (z == NZ - 1))
    def _():
        edge_copy(0, 1).wait()

    for i in range(KB):
        slots = []
        if i == 0:
            slots.append(jnp.where(z == 0, EDGE, z * KB - 1))
        else:
            slots.append(z * KB + i - 1)
        slots.append(z * KB + i)
        if i == KB - 1:
            slots.append(jnp.where(z == NZ - 1, EDGE, z * KB + KB))
        else:
            slots.append(z * KB + i + 1)
        for g in range(2):
            slots.append(jnp.where(x == 0, g, GLOB + g))
        for e in range(5, LIST):
            block = list_ref[i, e]
            shard = (block * 21846) >> 16
            here = (shard >> 4) == x
            slots.append(jnp.where(here, (shard & 15) * KB + block - shard * KB, RECV + shard))
        for e in range(LIST):
            again = jnp.int32(0)
            for f in range(e):
                again = again | jnp.where(list_ref[i, e] == list_ref[i, f], 1, 0)
            keep = jnp.where(again == 1, 0.0, 1.0)
            both = kv[slots[e]]
            kcat[i, pl.ds(e * BLOCK, BLOCK)] = both[:BLOCK]
            mask = jnp.full((BLOCK, HEAD_DIM), keep, jnp.float32).astype(jnp.bfloat16)
            vcat[i, pl.ds(e * BLOCK, BLOCK), pl.ds(0, HEAD_DIM)] = both[BLOCK:] * mask
            vcat[i, pl.ds(e * BLOCK, BLOCK), pl.ds(HEAD_DIM, HEAD_DIM)] = mask

    factor = math.log2(math.e) / math.sqrt(HEAD_DIM)

    def out_copy(d, step):
        t = lax.rem(p + d, NDP)
        return send(
            obuf.at[pl.ds(pl.multiple_of(t * TOK, 16), TOK), pl.ds(pl.multiple_of(step * PAIR * HEAD_DIM, 256), PAIR * HEAD_DIM)],
            out_ref.at[:, pl.ds(pl.multiple_of(p * WIDTH + step * PAIR * HEAD_DIM, 256), PAIR * HEAD_DIM)],
            out_send, out_recv, at_p(d))

    @pl.loop(0, STEPS)
    def _(step):
        for i in range(KB):
            tok = pl.ds(i * BLOCK, BLOCK)
            cols = [pl.ds(pl.multiple_of((step * PAIR + h) * HEAD_DIM, HEAD_DIM), HEAD_DIM) for h in range(PAIR)]
            q = jnp.concatenate([qbuf[tok, col] for col in cols], axis=0)
            scores = lax.dot_general(q, kcat[i], (((1,), (1,)), ((), ())), preferred_element_type=jnp.float32)
            row_max = jnp.max(scores, axis=-1, keepdims=True)
            unnormed = jnp.exp2((scores - row_max) * factor).astype(jnp.bfloat16)
            result = jnp.dot(unnormed, vcat[i], preferred_element_type=jnp.float32)
            result = (result[:, :HEAD_DIM] / result[:, HEAD_DIM:]).astype(jnp.bfloat16)
            for h in range(PAIR):
                obuf[tok, cols[h]] = result[h * BLOCK:(h + 1) * BLOCK]
        for d in range(1, NDP):
            out_copy(d, step).start()

    own_out = pltpu.make_async_copy(
        obuf.at[pl.ds(pl.multiple_of(p * TOK, 16), TOK)],
        out_ref.at[:, pl.ds(pl.multiple_of(p * WIDTH, WIDTH), WIDTH)], own_out_sem)
    own_out.start()
    own_out.wait()

    for way in range(2):
        up = way == 0
        dev = at_z(1 if up else NZ - 1)
        full = kv.at[pl.ds(0, (NZ // 2 - 1) * KB)]
        send(full, full, z_send.at[way], z_recv.at[way, 1, 0], dev).wait_send()
        half = kv.at[pl.ds(0, KB), pl.ds(0, BLOCK)]
        send(half, half, z_half_send.at[way], z_recv.at[way, 1, 0], dev).wait_send()

    @pl.when(x == 0)
    def _():
        for d in range(1, NX):
            glob_copy(d).wait_send()

    everything = out_ref.at[:, pl.ds(0, (NDP - 1) * WIDTH)]
    send(everything, everything, out_send, out_recv, at_p(1)).wait()


def shards(queries, keys, values, block_list):
    dma = pltpu.SemaphoreType.DMA
    bf16 = jnp.bfloat16
    hbm = pl.BlockSpec(memory_space=pl.ANY)
    return pl.pallas_call(
        kernel,
        out_shape=jax.ShapeDtypeStruct(queries.shape, queries.dtype),
        in_specs=[pl.BlockSpec(memory_space=pltpu.SMEM), hbm, hbm, hbm],
        out_specs=hbm,
        scratch_shapes=[
            pltpu.VMEM((SLOTS, 2 * BLOCK, HEAD_DIM), bf16),
            pltpu.VMEM((NX - 1, NZ, 2 * BLOCK, HEAD_DIM), bf16),
            pltpu.VMEM((KB, LIST * BLOCK, HEAD_DIM), bf16),
            pltpu.VMEM((KB, LIST * BLOCK, 2 * HEAD_DIM), bf16),
            pltpu.VMEM((SPAN, WIDTH), bf16),
            pltpu.VMEM((SPAN, WIDTH), bf16),
            pltpu.VMEM((NX, NZ, 128), jnp.int32),
            pltpu.VMEM((NX, NZ, 128), jnp.int32),
            pltpu.SMEM((NX, NZ, 128), jnp.int32),
            dma((2, KB)), dma, dma, dma((NX,)), dma((NX,)), dma, dma((NDP,)), dma((NDP,)),
            dma((2,)), dma((2,)), dma((2, NZ // 2, KB)), dma((2, KB)),
            dma((NX - 1,)), dma((NX - 1,)), dma((NX,)), dma, dma, dma, dma, dma,
        ],
        compiler_params=pltpu.CompilerParams(
            collective_id=0, has_side_effects=True, vmem_limit_bytes=48 * 1024 * 1024
        ),
        name="gather_attend",
    )(block_list, queries, keys.reshape(KB, BLOCK, HEAD_DIM), values.reshape(KB, BLOCK, HEAD_DIM))


def solution(mesh):
    in_specs = (P(("ctx", "dp"), None), P("ctx", "dp"), P("ctx", "dp"), P("ctx", None))
    out_specs = P(("ctx", "dp"), None)
    return jax.shard_map(shards, mesh=mesh, in_specs=in_specs, out_specs=out_specs, check_vma=False)
```

```python
import math

import jax
import jax.numpy as jnp
from jax import lax
from jax.experimental import pallas as pl
from jax.experimental.pallas import tpu as pltpu
from jax.sharding import PartitionSpec as P

HEAD_DIM = 128
BLOCK = 128
LIST = 13
KB = 3
GROUP = 8
NX, NZ, NDP = 4, 16, 8
TOK = 48
WIDTH = GROUP * HEAD_DIM
SPAN = KB * BLOCK
OWN = NZ * KB
RECV = OWN
GLOB = RECV + NX * NZ
EDGE = GLOB + 2
NEAR = 2
OPP = EDGE + 1
SLOTS = OPP + (2 * NEAR + 1) * KB
PAIR = 2
STEPS = GROUP // PAIR
MESH = pl.DeviceIdType.MESH


def kernel(list_ref, q_ref, k_ref, v_ref, out_ref, kv, picked, kcat, vcat, qbuf, obuf, ask, asked, asked_s, lower_in,
           load_sem, own_q_sem, own_out_sem, ask_send, ask_recv, asked_sem, q_send, q_recv, z_send, z_half_send, z_recv,
           z_half_recv, x_send, x_recv, glob_send, glob_recv, opp_send, opp_recv, edge_send, edge_recv, out_send, out_recv):
    c = lax.axis_index("ctx")
    p = lax.axis_index("dp")
    x = c // NZ
    z = c % NZ

    def at_x(d):
        return {"ctx": lax.rem(x + d, NX) * NZ + z, "dp": p}

    def at_z(d):
        return {"ctx": x * NZ + lax.rem(z + d, NZ), "dp": p}

    def at_p(d):
        return {"ctx": c, "dp": lax.rem(p + d, NDP)}

    def send(src, dst, ssem, rsem, dev):
        return pltpu.make_async_remote_copy(
            src_ref=src, dst_ref=dst, send_sem=ssem, recv_sem=rsem, device_id=dev, device_id_type=MESH
        )

    barrier = pltpu.get_barrier_semaphore()
    for d in range(1, NX):
        pl.semaphore_signal(barrier, inc=1, device_id=at_x(d), device_id_type=MESH)
    pl.semaphore_signal(barrier, inc=1, device_id=at_z(NZ - 1), device_id_type=MESH)
    for d in range(1, NDP):
        pl.semaphore_signal(barrier, inc=1, device_id=at_p(d), device_id_type=MESH)

    loads = []
    for b in range(KB):
        slot = z * KB + b
        loads.append(pltpu.make_async_copy(k_ref.at[b], kv.at[slot, pl.ds(0, BLOCK)], load_sem.at[0, b]))
        loads.append(pltpu.make_async_copy(v_ref.at[b], kv.at[slot, pl.ds(BLOCK, BLOCK)], load_sem.at[1, b]))
    for copy in loads:
        copy.start()
    own_q = pltpu.make_async_copy(
        q_ref.at[:, pl.ds(pl.multiple_of(p * WIDTH, WIDTH), WIDTH)],
        qbuf.at[pl.ds(pl.multiple_of(p * TOK, 16), TOK)], own_q_sem)
    own_q.start()

    rows = lax.broadcasted_iota(jnp.int32, (NX * NZ, 128), 0) * KB
    wanted = jnp.zeros((NX * NZ, 128), jnp.int32)
    for i in range(KB):
        for e in range(5, LIST):
            off = list_ref[i, e] - rows
            wanted = wanted + jnp.where(off == 1, 1, 0) + jnp.where(off == 2, 2, 0)
    ask[...] = wanted.reshape(NX, NZ, 128)

    for copy in loads:
        copy.wait()
    pl.semaphore_wait(barrier, NX - 1 + 1 + NDP - 1)
    pl.semaphore_signal(lower_in, inc=1, device_id=at_z(1), device_id_type=MESH)

    asks = []
    for d in range(1, NX):
        asks.append(send(ask.at[lax.rem(x + d, NX)], asked.at[d], ask_send.at[d], ask_recv.at[d], at_x(d)))
        asks[-1].start()

    def z_block(slot, up, k, b):
        way = 0 if up else 1
        s = slot * KB + b
        return send(kv.at[s], kv.at[s], z_send.at[way], z_recv.at[way, k, b], at_z(1 if up else NZ - 1))

    def z_half(slot, up, b):
        way = 0 if up else 1
        s = slot * KB + b
        part = pl.ds(0 if up else BLOCK, BLOCK)
        return send(kv.at[s, part], kv.at[s, part], z_half_send.at[way], z_half_recv.at[way, b],
                    at_z(1 if up else NZ - 1))

    for b in range(KB):
        z_block(z, True, 1, b).start()

    def opp_block(way, hop, b):
        row = -hop if way == 0 else hop
        step = -1 if way == 0 else 1
        return send(kv.at[OPP + (row + NEAR) * KB + b], kv.at[OPP + (row + step + NEAR) * KB + b],
                    opp_send.at[way], opp_recv.at[way, hop + 1, b], at_z(1 if way == 0 else NZ - 1))

    def opp_first(b):
        return send(kv.at[z * KB + b], kv.at[OPP + NEAR * KB + b], opp_send.at[2], opp_recv.at[0, 0, b], at_x(2))

    for b in range(KB):
        opp_first(b).start()

    q_copies = []
    for d in range(1, NDP):
        t = lax.rem(p + d, NDP)
        q_copies.append(send(
            q_ref.at[:, pl.ds(pl.multiple_of(t * WIDTH, WIDTH), WIDTH)],
            qbuf.at[pl.ds(pl.multiple_of(p * TOK, 16), TOK)],
            q_send.at[d], q_recv.at[d], at_p(d)))
        q_copies[-1].start()

    def start_down():
        pl.semaphore_wait(lower_in, 1)
        for b in range(KB):
            z_block(z, False, 1, b).start()

    pl.when(z != 0)(start_down)

    for copy in asks:
        copy.wait()
    to_scalars = pltpu.make_async_copy(asked, asked_s, asked_sem)
    to_scalars.start()
    to_scalars.wait()

    def glob_copy(d):
        return send(kv.at[pl.ds(0, 2)], kv.at[pl.ds(GLOB, 2)], glob_send.at[d], glob_recv, at_x(d))

    def glob_on(way):
        both = kv.at[pl.ds(GLOB, 2)]
        return send(both, both, glob_send.at[way], glob_recv, at_z(1 if way == 0 else NZ - 1))

    up_on = (x != 0) & (z < NZ // 2)
    down_on = (x != 0) & ((z == 0) | (z > NZ // 2 + 1))

    def edge_copy(slot, d):
        return send(kv.at[slot], kv.at[EDGE], edge_send, edge_recv, at_x(d))

    def share(slot, dests, edges=True):
        first, second, third = (kv[slot * KB + b] for b in range(KB))

        def give(d):
            off = asked_s[NX - d, slot, 0]
            picked[d - 1, slot] = jnp.where(off == 1, second, jnp.where(off == 2, third, first))
            send(picked.at[d - 1, slot], kv.at[RECV + x * NZ + slot], x_send.at[d - 1], x_recv.at[d - 1],
                 at_x(d)).start()

        for d in dests:
            give(d)
        if not edges:
            return

        @pl.when((z == 0) & (slot == NZ - 1))
        def _():
            edge_copy((NZ - 1) * KB + KB - 1, 1).start()

        @pl.when((z == NZ - 1) & (slot == 0))
        def _():
            edge_copy(0, NX - 1).start()

    @pl.when((x == 0) & (z == 0))
    def _():
        for d in range(1, NX):
            glob_copy(d).start()

    share(z, (1, 3))
    pl.when(z == 0)(start_down)

    @pl.when((x != 0) & (z == 0))
    def _():
        glob_copy(1).wait_recv()
        glob_on(0).start()
        glob_on(1).start()

    @pl.loop(1, NZ // 2)
    def _(k):
        above = lax.rem(z + NZ - k, NZ)
        below = lax.rem(z + k, NZ)
        for b in range(KB):
            for up, slot in ((True, above), (False, below)):
                z_block(slot, up, k, b).wait_recv()

                @pl.when(k < NZ // 2 - 1)
                def _():
                    z_block(slot, up, k + 1, b).start()

                @pl.when(k == NZ // 2 - 1)
                def _():
                    z_half(slot, up, b).start()

        @pl.when((x != 0) & ((above == 0) | (below == 0)) & (z != NZ // 2))
        def _():
            glob_copy(1).wait_recv()
            pl.when(up_on)(lambda: glob_on(0).start())
            pl.when(down_on)(lambda: glob_on(1).start())

        @pl.when(k <= NEAR)
        def _():
            share(above, (1, 3))

        @pl.when(k > NEAR)
        def _():
            share(above, (2, 1, 3))

        share(below, (1, 3))

    for b in range(KB):
        opp_first(b).wait_recv()
        for way in range(2):
            opp_block(way, 0, b).start()

    far = lax.rem(z + NZ // 2, NZ)
    for b in range(KB):
        for up in (True, False):
            z_half(far, up, b).wait_recv()
    share(far, (1, 3, 2))

    for hop in range(1, NEAR):
        for b in range(KB):
            for way in range(2):
                opp_block(way, hop - 1, b).wait_recv()
                opp_block(way, hop, b).start()

    @pl.loop(NEAR + 1, NZ // 2)
    def _(k):
        share(lax.rem(z + k, NZ), (2,), False)

    for copy in q_copies:
        copy.wait()
    own_q.wait()

    for d in range(1, NX):
        source = lax.rem(x + NX - d, NX)
        count = NZ if d != 2 else NZ - 2 * NEAR - 1
        landed = kv.at[pl.ds(RECV + source * NZ, count)]
        send(picked.at[d - 1, pl.ds(0, count)], landed, x_send.at[d - 1], x_recv.at[d - 1], at_x(d)).wait()

    for way in range(2):
        for b in range(KB):
            opp_block(way, NEAR - 1, b).wait_recv()

    @pl.when((x != 0) & (z == NZ // 2))
    def _():
        glob_copy(1).wait_recv()

    @pl.when((z == 0) | (z == NZ - 1))
    def _():
        edge_copy(0, 1).wait()

    for i in range(KB):
        slots = []
        if i == 0:
            slots.append(jnp.where(z == 0, EDGE, z * KB - 1))
        else:
            slots.append(z * KB + i - 1)
        slots.append(z * KB + i)
        if i == KB - 1:
            slots.append(jnp.where(z == NZ - 1, EDGE, z * KB + KB))
        else:
            slots.append(z * KB + i + 1)
        for g in range(2):
            slots.append(jnp.where(x == 0, g, GLOB + g))
        for e in range(5, LIST):
            block = list_ref[i, e]
            shard = (block * 21846) >> 16
            column, row, off = shard >> 4, shard & (NZ - 1), block - shard * KB
            ahead = ((row - z + NZ + NEAR) & (NZ - 1))
            near = (column == lax.rem(x + 2, NX)) & (ahead <= 2 * NEAR)
            slot = jnp.where(near, OPP + ahead * KB + off, RECV + shard)
            slots.append(jnp.where(column == x, row * KB + off, slot))
        for e in range(LIST):
            again = jnp.int32(0)
            for f in range(e):
                again = again | jnp.where(list_ref[i, e] == list_ref[i, f], 1, 0)
            keep = jnp.where(again == 1, 0.0, 1.0)
            both = kv[slots[e]]
            kcat[i, pl.ds(e * BLOCK, BLOCK)] = both[:BLOCK]
            mask = jnp.full((BLOCK, HEAD_DIM), keep, jnp.float32).astype(jnp.bfloat16)
            vcat[i, pl.ds(e * BLOCK, BLOCK), pl.ds(0, HEAD_DIM)] = both[BLOCK:] * mask
            vcat[i, pl.ds(e * BLOCK, BLOCK), pl.ds(HEAD_DIM, HEAD_DIM)] = mask

    factor = math.log2(math.e) / math.sqrt(HEAD_DIM)

    def out_copy(d, step):
        t = lax.rem(p + d, NDP)
        return send(
            obuf.at[pl.ds(pl.multiple_of(t * TOK, 16), TOK), pl.ds(pl.multiple_of(step * PAIR * HEAD_DIM, 256), PAIR * HEAD_DIM)],
            out_ref.at[:, pl.ds(pl.multiple_of(p * WIDTH + step * PAIR * HEAD_DIM, 256), PAIR * HEAD_DIM)],
            out_send, out_recv, at_p(d))

    @pl.loop(0, STEPS)
    def _(step):
        for i in range(KB):
            tok = pl.ds(i * BLOCK, BLOCK)
            cols = [pl.ds(pl.multiple_of((step * PAIR + h) * HEAD_DIM, HEAD_DIM), HEAD_DIM) for h in range(PAIR)]
            q = jnp.concatenate([qbuf[tok, col] for col in cols], axis=0)
            scores = lax.dot_general(q, kcat[i], (((1,), (1,)), ((), ())), preferred_element_type=jnp.float32)
            row_max = jnp.max(scores, axis=-1, keepdims=True)
            unnormed = jnp.exp2((scores - row_max) * factor).astype(jnp.bfloat16)
            result = jnp.dot(unnormed, vcat[i], preferred_element_type=jnp.float32)
            result = (result[:, :HEAD_DIM] / result[:, HEAD_DIM:]).astype(jnp.bfloat16)
            for h in range(PAIR):
                obuf[tok, cols[h]] = result[h * BLOCK:(h + 1) * BLOCK]
        for d in range(1, NDP):
            out_copy(d, step).start()

    own_out = pltpu.make_async_copy(
        obuf.at[pl.ds(pl.multiple_of(p * TOK, 16), TOK)],
        out_ref.at[:, pl.ds(pl.multiple_of(p * WIDTH, WIDTH), WIDTH)], own_out_sem)
    own_out.start()
    own_out.wait()

    opp_blocks = kv.at[pl.ds(0, NEAR * KB)]
    own_blocks = kv.at[pl.ds(0, KB)]
    for way in range(2):
        send(opp_blocks, opp_blocks, opp_send.at[way], out_recv, at_z(1 if way == 0 else NZ - 1)).wait_send()
    send(own_blocks, own_blocks, opp_send.at[2], out_recv, at_x(2)).wait_send()
    for way in range(2):
        up = way == 0
        dev = at_z(1 if up else NZ - 1)
        full = kv.at[pl.ds(0, (NZ // 2 - 1) * KB)]
        send(full, full, z_send.at[way], z_recv.at[way, 1, 0], dev).wait_send()
        half = kv.at[pl.ds(0, KB), pl.ds(0, BLOCK)]
        send(half, half, z_half_send.at[way], z_recv.at[way, 1, 0], dev).wait_send()

    @pl.when((x == 0) & (z == 0))
    def _():
        for d in range(1, NX):
            glob_copy(d).wait_send()

    pl.when(up_on)(lambda: glob_on(0).wait_send())
    pl.when(down_on)(lambda: glob_on(1).wait_send())

    everything = out_ref.at[:, pl.ds(0, (NDP - 1) * WIDTH)]
    send(everything, everything, out_send, out_recv, at_p(1)).wait()


def shards(queries, keys, values, block_list):
    dma = pltpu.SemaphoreType.DMA
    bf16 = jnp.bfloat16
    hbm = pl.BlockSpec(memory_space=pl.ANY)
    return pl.pallas_call(
        kernel,
        out_shape=jax.ShapeDtypeStruct(queries.shape, queries.dtype),
        in_specs=[pl.BlockSpec(memory_space=pltpu.SMEM), hbm, hbm, hbm],
        out_specs=hbm,
        scratch_shapes=[
            pltpu.VMEM((SLOTS, 2 * BLOCK, HEAD_DIM), bf16),
            pltpu.VMEM((NX - 1, NZ, 2 * BLOCK, HEAD_DIM), bf16),
            pltpu.VMEM((KB, LIST * BLOCK, HEAD_DIM), bf16),
            pltpu.VMEM((KB, LIST * BLOCK, 2 * HEAD_DIM), bf16),
            pltpu.VMEM((SPAN, WIDTH), bf16),
            pltpu.VMEM((SPAN, WIDTH), bf16),
            pltpu.VMEM((NX, NZ, 128), jnp.int32),
            pltpu.VMEM((NX, NZ, 128), jnp.int32),
            pltpu.SMEM((NX, NZ, 128), jnp.int32),
            pltpu.SemaphoreType.REGULAR,
            dma((2, KB)), dma, dma, dma((NX,)), dma((NX,)), dma, dma((NDP,)), dma((NDP,)),
            dma((2,)), dma((2,)), dma((2, NZ // 2, KB)), dma((2, KB)),
            dma((NX - 1,)), dma((NX - 1,)), dma((NX,)), dma, dma((3,)), dma((2, NEAR + 1, KB)), dma, dma, dma, dma,
        ],
        compiler_params=pltpu.CompilerParams(
            collective_id=0, has_side_effects=True, vmem_limit_bytes=63 * 1024 * 1024
        ),
        name="gather_attend",
    )(block_list, queries, keys.reshape(KB, BLOCK, HEAD_DIM), values.reshape(KB, BLOCK, HEAD_DIM))


def solution(mesh):
    in_specs = (P(("ctx", "dp"), None), P("ctx", "dp"), P("ctx", "dp"), P("ctx", None))
    out_specs = P(("ctx", "dp"), None)
    return jax.shard_map(shards, mesh=mesh, in_specs=in_specs, out_specs=out_specs, check_vma=False)
```

```python
import math

import jax
import jax.numpy as jnp
from jax import lax
from jax.experimental import pallas as pl
from jax.experimental.pallas import tpu as pltpu
from jax.sharding import PartitionSpec as P

HEAD_DIM = 128
BLOCK = 128
LIST = 13
KB = 3
GROUP = 8
NX, NZ, NDP = 4, 16, 8
TOK = 48
WIDTH = GROUP * HEAD_DIM
SPAN = KB * BLOCK
OWN = NZ * KB
RECV = OWN
GLOB = RECV + NX * NZ
EDGE = GLOB + 2
OPP_AT = (5, 7)
OWN_PLACE, FAR_PLACE = NZ - 2, NZ - 1
GLOB_LAG = 2
NEAR = 2
OPP = EDGE + 1
SLOTS = OPP + (2 * NEAR + 1) * KB
PAIR = 2
STEPS = GROUP // PAIR
MESH = pl.DeviceIdType.MESH


def kernel(list_ref, q_ref, k_ref, v_ref, out_ref, kv, picked, kcat, vcat, qbuf, obuf, ask, asked, asked_s, lower_in,
           load_sem, own_q_sem, own_out_sem, ask_send, ask_recv, asked_sem, q_send, q_recv, z_send, z_recv, x_send, x_recv,
           glob_send, glob_recv, opp_send, opp_recv, edge_send, edge_recv, out_send, out_recv):
    c = lax.axis_index("ctx")
    p = lax.axis_index("dp")
    x = c // NZ
    z = c & (NZ - 1)
    at_x = [{"ctx": ((x + d) & (NX - 1)) * NZ + z, "dp": p} for d in range(NX)]
    at_z = [{"ctx": x * NZ + ((z + d) & (NZ - 1)), "dp": p} for d in (1, NZ - 1)]
    others = [(p + d) & (NDP - 1) for d in range(NDP)]
    at_p = [{"ctx": c, "dp": t} for t in others]

    def send(src, dst, ssem, rsem, dev):
        return pltpu.make_async_remote_copy(
            src_ref=src, dst_ref=dst, send_sem=ssem, recv_sem=rsem, device_id=dev, device_id_type=MESH
        )

    def blocks(slot, count):
        return kv.at[pl.ds(2 * slot, 2 * count)]

    barrier = pltpu.get_barrier_semaphore()
    for dev in at_x[1:] + at_z[1:] + at_p[1:]:
        pl.semaphore_signal(barrier, inc=1, device_id=dev, device_id_type=MESH)

    loads = []
    for b in range(KB):
        part = 2 * (z * KB + b)
        loads.append(pltpu.make_async_copy(k_ref.at[b], kv.at[part], load_sem.at[0, b]))
        loads.append(pltpu.make_async_copy(v_ref.at[b], kv.at[part + 1], load_sem.at[1, b]))
    for copy in loads:
        copy.start()
    own_rows = pl.ds(pl.multiple_of(p * TOK, 16), TOK)
    own_q = pltpu.make_async_copy(
        q_ref.at[:, pl.ds(pl.multiple_of(p * WIDTH, WIDTH), WIDTH)], qbuf.at[own_rows], own_q_sem)
    own_q.start()

    rows = lax.broadcasted_iota(jnp.int32, (NX * NZ, 128), 0) * KB
    wanted = jnp.zeros((NX * NZ, 128), jnp.int32)
    for i in range(KB):
        for e in range(5, LIST):
            off = list_ref[i, e] - rows
            wanted = wanted + jnp.where(off == 1, 1, 0) + jnp.where(off == 2, 2, 0)
    ask[...] = wanted.reshape(NX, NZ, 128)

    for copy in loads:
        copy.wait()
    pl.semaphore_wait(barrier, NX - 1 + 1 + NDP - 1)
    pl.semaphore_signal(lower_in, inc=1, device_id=at_z[0], device_id_type=MESH)

    def z_part(slot, way, k, part):
        half = kv.at[pl.ds(2 * KB * slot + KB * part, KB)]
        return send(half, half, z_send.at[way], z_recv.at[way, k - 1, part], at_z[way])

    for part in range(2):
        z_part(z, 0, 1, part).start()

    asks = []
    for d in range(1, NX):
        asks.append(send(ask.at[(x + d) & (NX - 1)], asked.at[d], ask_send.at[d], ask_recv.at[d], at_x[d]))
        asks[-1].start()

    def opp_shard(way, hop):
        row, step = (-hop, -1) if way == 0 else (hop, 1)
        return send(blocks(OPP + (row + NEAR) * KB, KB), blocks(OPP + (row + step + NEAR) * KB, KB),
                    opp_send.at[way], opp_recv.at[way, hop + 1], at_z[way])

    opp_first = send(blocks(z * KB, KB), blocks(OPP + NEAR * KB, KB), opp_send.at[2], opp_recv.at[0, 0], at_x[2])
    opp_first.start()

    def start_down():
        pl.semaphore_wait(lower_in, 1)
        for part in (1, 0):
            z_part(z, 1, 1, part).start()

    pl.when(z != 0)(start_down)

    for copy in asks:
        copy.wait()
    to_scalars = pltpu.make_async_copy(asked, asked_s, asked_sem)
    to_scalars.start()

    q_copies = []
    for d in range(1, NDP):
        q_copies.append(send(
            q_ref.at[:, pl.ds(pl.multiple_of(others[d] * WIDTH, WIDTH), WIDTH)], qbuf.at[own_rows],
            q_send.at[d], q_recv.at[d], at_p[d]))
        q_copies[-1].start()

    def glob_copy(d, g):
        return send(blocks(g, 1), blocks(GLOB + g, 1), glob_send.at[d], glob_recv.at[g], at_x[d])

    def glob_on(way, g):
        one = blocks(GLOB + g, 1)
        return send(one, one, glob_send.at[way], glob_recv.at[g], at_z[way])

    hops = jnp.where(z > NZ // 2, NZ - z, z)
    up_on = (x != 0) & (z < NZ // 2)
    down_on = (x != 0) & ((z == 0) | (z > NZ // 2 + 1))

    def glob_pass():
        for g in range(2):
            glob_on(0, g).wait_recv()
            pl.when(up_on)(lambda: glob_on(0, g).start())
            pl.when(down_on)(lambda: glob_on(1, g).start())

    def edge_copy(slot, d):
        return send(blocks(slot, 1), blocks(EDGE, 1), edge_send, edge_recv, at_x[d])

    def pick(slot, d, place):
        first, second, third = (kv[pl.ds(2 * (slot * KB + b), 2)] for b in range(KB))
        off = asked_s[NX - d, slot, 0]
        picked[d - 1, pl.ds(2 * place, 2)] = jnp.where(off == 1, second, jnp.where(off == 2, third, first))

    def give(d, place, count):
        send(picked.at[d - 1, pl.ds(2 * place, 2 * count)], blocks(RECV + x * NZ + place, count),
             x_send.at[d - 1], x_recv.at[d - 1], at_x[d]).start()

    to_scalars.wait()

    @pl.when((x == 0) & (z == 0))
    def _():
        for g in range(2):
            for d in range(1, NX):
                glob_copy(d, g).start()

    for d in (1, 3):
        pick(z, d, OWN_PLACE)
        give(d, OWN_PLACE, 1)
    pl.when(z == 0)(start_down)

    @pl.loop(1, NZ // 2)
    def _(k):
        slots = ((z + NZ - k) & (NZ - 1), (z + k) & (NZ - 1))
        for turn in range(2):
            for way in range(2):
                part = turn if way == 0 else 1 - turn
                z_part(slots[way], way, k, part).wait_recv()
                if part == way:
                    z_part(slots[way], way, k + 1, part).start()
                else:
                    pl.when(k < NZ // 2 - 1)(lambda: z_part(slots[way], way, k + 1, part).start())

        def share(d):
            for way in range(2):
                pick(slots[way], d, 2 * (k - 1) + way)
            give(d, 2 * (k - 1), 2)

        pl.when(k > NEAR)(lambda: share(2))
        share(1)
        share(3)

        @pl.when((z == 0) & (k == 1))
        def _():
            edge_copy(OWN - 1, 1).start()

        @pl.when((z == NZ - 1) & (k == 1))
        def _():
            edge_copy(0, NX - 1).start()

        pl.when((x != 0) & (hops == k - GLOB_LAG))(glob_pass)

        for hop in range(NEAR):
            @pl.when(k == OPP_AT[hop])
            def _():
                if hop == 0:
                    opp_first.wait_recv()
                for way in range(2):
                    if hop > 0:
                        opp_shard(way, hop - 1).wait_recv()
                    opp_shard(way, hop).start()

    far = (z + NZ // 2) & (NZ - 1)
    for way in range(2):
        z_part(far, way, NZ // 2, way).wait_recv()
    for d in (2, 1, 3):
        pick(far, d, FAR_PLACE)
        give(d, FAR_PLACE, 1)
    pl.when((x != 0) & (hops > NZ // 2 - 1 - GLOB_LAG))(glob_pass)

    for copy in q_copies:
        copy.wait()
    own_q.wait()

    for d in (1, 3, 2):
        count = NZ if d != 2 else NZ - 2 * NEAR - 1
        landed = blocks(RECV + ((x - d) & (NX - 1)) * NZ, count)
        send(picked.at[d - 1, pl.ds(0, 2 * count)], landed, x_send.at[d - 1], x_recv.at[d - 1], at_x[d]).wait()

    if NEAR:
        for way in range(2):
            opp_shard(way, NEAR - 1).wait_recv()
    else:
        opp_first.wait_recv()

    @pl.when((z == 0) | (z == NZ - 1))
    def _():
        edge_copy(0, 1).wait()

    for i in range(KB):
        slots = []
        if i == 0:
            slots.append(jnp.where(z == 0, EDGE, z * KB - 1))
        else:
            slots.append(z * KB + i - 1)
        slots.append(z * KB + i)
        if i == KB - 1:
            slots.append(jnp.where(z == NZ - 1, EDGE, z * KB + KB))
        else:
            slots.append(z * KB + i + 1)
        for g in range(2):
            slots.append(jnp.where(x == 0, g, GLOB + g))
        for e in range(5, LIST):
            block = list_ref[i, e]
            shard = (block * 21846) >> 16
            column, row, off = shard >> 4, shard & (NZ - 1), block - shard * KB
            ahead = ((row - z + NZ + NEAR) & (NZ - 1))
            ahead = (row - z) & (NZ - 1)
            place = jnp.where(ahead > NZ // 2, 2 * (NZ - 1 - ahead), 2 * ahead - 1)
            place = jnp.where(ahead == 0, OWN_PLACE, jnp.where(ahead == NZ // 2, FAR_PLACE, place))
            ahead = (ahead + NEAR) & (NZ - 1)
            near = (column == ((x + 2) & (NX - 1))) & (ahead <= 2 * NEAR)
            slot = jnp.where(near, OPP + ahead * KB + off, RECV + column * NZ + place)
            slots.append(jnp.where(column == x, row * KB + off, slot))
        for e in range(LIST):
            again = jnp.int32(0)
            for f in range(e):
                again = again | jnp.where(list_ref[i, e] == list_ref[i, f], 1, 0)
            keep = jnp.where(again == 1, 0.0, 1.0)
            both = kv[pl.ds(2 * slots[e], 2)]
            kcat[i, pl.ds(e * BLOCK, BLOCK)] = both[0]
            mask = jnp.full((BLOCK, HEAD_DIM), keep, jnp.float32).astype(jnp.bfloat16)
            vcat[i, pl.ds(e * BLOCK, BLOCK), pl.ds(0, HEAD_DIM)] = both[1] * mask
            vcat[i, pl.ds(e * BLOCK, BLOCK), pl.ds(HEAD_DIM, HEAD_DIM)] = mask

    factor = math.log2(math.e) / math.sqrt(HEAD_DIM)

    def out_copy(d, step):
        return send(
            obuf.at[pl.ds(pl.multiple_of(others[d] * TOK, 16), TOK), pl.ds(pl.multiple_of(step * PAIR * HEAD_DIM, 256), PAIR * HEAD_DIM)],
            out_ref.at[:, pl.ds(pl.multiple_of(p * WIDTH + step * PAIR * HEAD_DIM, 256), PAIR * HEAD_DIM)],
            out_send, out_recv, at_p[d])

    @pl.loop(0, STEPS)
    def _(step):
        for i in range(KB):
            tok = pl.ds(i * BLOCK, BLOCK)
            cols = [pl.ds(pl.multiple_of((step * PAIR + h) * HEAD_DIM, HEAD_DIM), HEAD_DIM) for h in range(PAIR)]
            q = jnp.concatenate([qbuf[tok, col] for col in cols], axis=0)
            scores = lax.dot_general(q, kcat[i], (((1,), (1,)), ((), ())), preferred_element_type=jnp.float32)
            row_max = jnp.max(scores, axis=-1, keepdims=True)
            unnormed = jnp.exp2((scores - row_max) * factor).astype(jnp.bfloat16)
            result = jnp.dot(unnormed, vcat[i], preferred_element_type=jnp.float32)
            result = (result[:, :HEAD_DIM] / result[:, HEAD_DIM:]).astype(jnp.bfloat16)
            for h in range(PAIR):
                obuf[tok, cols[h]] = result[h * BLOCK:(h + 1) * BLOCK]
        for d in range(1, NDP):
            out_copy(d, step).start()

    own_out = pltpu.make_async_copy(
        obuf.at[pl.ds(pl.multiple_of(p * TOK, 16), TOK)],
        out_ref.at[:, pl.ds(pl.multiple_of(p * WIDTH, WIDTH), WIDTH)], own_out_sem)
    own_out.start()
    own_out.wait()

    for way in range(2):
        if NEAR:
            passed = blocks(0, NEAR * KB)
            send(passed, passed, opp_send.at[way], out_recv, at_z[way]).wait_send()
        sent = kv.at[pl.ds(0, (NZ - 1) * KB)]
        send(sent, sent, z_send.at[way], out_recv, at_z[way]).wait_send()
    opp_first.wait_send()

    @pl.when((x == 0) & (z == 0))
    def _():
        both = blocks(0, 2)
        for d in range(1, NX):
            send(both, both, glob_send.at[d], out_recv, at_x[d]).wait_send()

    def glob_sent(way):
        both = blocks(GLOB, 2)
        send(both, both, glob_send.at[way], out_recv, at_z[way]).wait_send()

    pl.when(up_on)(lambda: glob_sent(0))
    pl.when(down_on)(lambda: glob_sent(1))

    everything = out_ref.at[:, pl.ds(0, (NDP - 1) * WIDTH)]
    send(everything, everything, out_send, out_recv, at_p[1]).wait()


def shards(queries, keys, values, block_list):
    dma = pltpu.SemaphoreType.DMA
    bf16 = jnp.bfloat16
    hbm = pl.BlockSpec(memory_space=pl.ANY)
    return pl.pallas_call(
        kernel,
        out_shape=jax.ShapeDtypeStruct(queries.shape, queries.dtype),
        in_specs=[pl.BlockSpec(memory_space=pltpu.SMEM), hbm, hbm, hbm],
        out_specs=hbm,
        scratch_shapes=[
            pltpu.VMEM((2 * SLOTS, BLOCK, HEAD_DIM), bf16),
            pltpu.VMEM((NX - 1, 2 * NZ, BLOCK, HEAD_DIM), bf16),
            pltpu.VMEM((KB, LIST * BLOCK, HEAD_DIM), bf16),
            pltpu.VMEM((KB, LIST * BLOCK, 2 * HEAD_DIM), bf16),
            pltpu.VMEM((SPAN, WIDTH), bf16),
            pltpu.VMEM((SPAN, WIDTH), bf16),
            pltpu.VMEM((NX, NZ, 128), jnp.int32),
            pltpu.VMEM((NX, NZ, 128), jnp.int32),
            pltpu.SMEM((NX, NZ, 128), jnp.int32),
            pltpu.SemaphoreType.REGULAR,
            dma((2, KB)), dma, dma, dma((NX,)), dma((NX,)), dma, dma((NDP,)), dma((NDP,)),
            dma((2,)), dma((2, NZ // 2, 2)),
            dma((NX - 1,)), dma((NX - 1,)), dma((NX,)), dma((2,)), dma((3,)), dma((2, NEAR + 1)), dma, dma, dma, dma,
        ],
        compiler_params=pltpu.CompilerParams(
            collective_id=0, has_side_effects=True, vmem_limit_bytes=63 * 1024 * 1024
        ),
        name="gather_attend",
    )(block_list, queries, keys.reshape(KB, BLOCK, HEAD_DIM), values.reshape(KB, BLOCK, HEAD_DIM))


def solution(mesh):
    in_specs = (P(("ctx", "dp"), None), P("ctx", "dp"), P("ctx", "dp"), P("ctx", None))
    out_specs = P(("ctx", "dp"), None)
    return jax.shard_map(shards, mesh=mesh, in_specs=in_specs, out_specs=out_specs, check_vma=False)
```

```python
import math

import jax
import jax.numpy as jnp
from jax import lax
from jax.experimental import pallas as pl
from jax.experimental.pallas import tpu as pltpu
from jax.sharding import PartitionSpec as P

HEAD_DIM = 128
BLOCK = 128
LIST = 13
KB = 3
GROUP = 8
NX, NZ, NDP = 4, 16, 8
TOK = 48
WIDTH = GROUP * HEAD_DIM
SPAN = KB * BLOCK
OWN = NZ * KB
RECV = OWN
GLOB = RECV + NX * NZ
EDGE = GLOB + 2
OPP_AT = (5, 7)
OWN_PLACE, FAR_PLACE = NZ - 2, NZ - 1
GLOB_LAG = 2
LATE = 7
NEAR = 2
OPP = EDGE + 1
SLOTS = OPP + (2 * NEAR + 1) * KB
PAIR = 2
STEPS = GROUP // PAIR
MESH = pl.DeviceIdType.MESH


def kernel(lists, q_ref, k_ref, v_ref, out_ref, kv, given_v, picked, kcat, vcat, weights, qbuf, obuf, ask, asked, asked_s, list_ref, lower_in,
           list_sem, load_sem, own_q_sem, own_out_sem, ask_send, ask_recv, asked_sem, q_send, q_recv, z_send, z_recv, x_send, x_recv,
           glob_send, glob_recv, opp_send, opp_recv, edge_send, edge_recv, out_send, out_recv):
    c = lax.axis_index("ctx")
    p = lax.axis_index("dp")
    x = c // NZ
    z = c & (NZ - 1)
    at_x = [{"ctx": ((x + d) & (NX - 1)) * NZ + z, "dp": p} for d in range(NX)]
    at_z = [{"ctx": x * NZ + ((z + d) & (NZ - 1)), "dp": p} for d in (1, NZ - 1)]
    others = [(p + d) & (NDP - 1) for d in range(NDP)]
    at_p = [{"ctx": c, "dp": t} for t in others]

    def send(src, dst, ssem, rsem, dev):
        return pltpu.make_async_remote_copy(
            src_ref=src, dst_ref=dst, send_sem=ssem, recv_sem=rsem, device_id=dev, device_id_type=MESH
        )

    def blocks(slot, count):
        return kv.at[pl.ds(slot, count)]

    list_copy = pltpu.make_async_copy(lists, list_ref, list_sem)
    list_copy.start()
    barrier = pltpu.get_barrier_semaphore()
    for dev in at_x[1:] + at_z[1:] + at_p[1:]:
        pl.semaphore_signal(barrier, inc=1, device_id=dev, device_id_type=MESH)

    loads = []
    for b in range(KB):
        loads.append(pltpu.make_async_copy(k_ref.at[b], kv.at[z * KB + b, 0], load_sem.at[0, b]))
        loads.append(pltpu.make_async_copy(v_ref.at[b], kv.at[z * KB + b, 1], load_sem.at[1, b]))
    for copy in loads:
        copy.start()
    own_rows = pl.ds(pl.multiple_of(p * TOK, 16), TOK)
    own_q = pltpu.make_async_copy(
        q_ref.at[:, pl.ds(pl.multiple_of(p * WIDTH, WIDTH), WIDTH)], qbuf.at[own_rows], own_q_sem)
    own_q.start()

    list_copy.wait()
    rows = lax.broadcasted_iota(jnp.int32, (NX * NZ, 128), 0) * KB
    wanted = jnp.zeros((NX * NZ, 128), jnp.int32)
    for i in range(KB):
        for e in range(5, LIST):
            off = list_ref[i, e] - rows
            wanted = wanted + jnp.where(off == 1, 1, 0) + jnp.where(off == 2, 2, 0)
    ask[...] = wanted.reshape(NX, NZ, 128)

    for copy in loads:
        copy.wait()
    pl.semaphore_wait(barrier, NX - 1 + 1 + NDP - 1)
    pl.semaphore_signal(lower_in, inc=1, device_id=at_z[0], device_id_type=MESH)

    def z_part(slot, way, k, part):
        half = kv.at[pl.ds(KB * slot, KB), part]
        return send(half, half, z_send.at[way], z_recv.at[way, k - 1, part], at_z[way])

    for part in range(2):
        z_part(z, 0, 1, part).start()

    asks = []
    for d in range(1, NX):
        asks.append(send(ask.at[(x + d) & (NX - 1)], asked.at[d], ask_send.at[d], ask_recv.at[d], at_x[d]))
        asks[-1].start()

    def opp_shard(way, hop):
        row, step = (-hop, -1) if way == 0 else (hop, 1)
        return send(blocks(OPP + (row + NEAR) * KB, KB), blocks(OPP + (row + step + NEAR) * KB, KB),
                    opp_send.at[way], opp_recv.at[way, hop + 1], at_z[way])

    opp_first = send(blocks(z * KB, KB), blocks(OPP + NEAR * KB, KB), opp_send.at[2], opp_recv.at[0, 0], at_x[2])
    opp_first.start()

    def start_down():
        pl.semaphore_wait(lower_in, 1)
        for part in (1, 0):
            z_part(z, 1, 1, part).start()

    pl.when(z != 0)(start_down)

    for copy in asks:
        copy.wait()
    to_scalars = pltpu.make_async_copy(asked, asked_s, asked_sem)
    to_scalars.start()

    def glob_copy(d, g):
        return send(blocks(g, 1), blocks(GLOB + g, 1), glob_send.at[d], glob_recv.at[g], at_x[d])

    def glob_on(way, g):
        one = blocks(GLOB + g, 1)
        return send(one, one, glob_send.at[way], glob_recv.at[g], at_z[way])

    hops = jnp.where(z > NZ // 2, NZ - z, z)
    up_on = (x != 0) & (z < NZ // 2)
    down_on = (x != 0) & ((z == 0) | (z > NZ // 2 + 1))

    def glob_pass():
        for g in range(2):
            glob_on(0, g).wait_recv()
            pl.when(up_on)(lambda: glob_on(0, g).start())
            pl.when(down_on)(lambda: glob_on(1, g).start())

    def edge_copy(slot, d):
        return send(blocks(slot, 1), blocks(EDGE, 1), edge_send, edge_recv, at_x[d])

    def pick(slot, d, place):
        first, second, third = (kv[slot * KB + b] for b in range(KB))
        off = asked_s[NX - d, slot, 0]
        picked[d - 1, place] = jnp.where(off == 1, second, jnp.where(off == 2, third, first))

    def give(d, place, count, parts=(0, 1)):
        for part in parts:
            if part == 0:
                target = kv.at[pl.ds(RECV + x * NZ + place, count), 0]
            else:
                target = given_v.at[pl.ds(x * NZ + place, count)]
            send(picked.at[d - 1, pl.ds(place, count), part], target,
                 x_send.at[part, d - 1], x_recv.at[part, d - 1], at_x[d]).start()

    to_scalars.wait()

    @pl.when((x == 0) & (z == 0))
    def _():
        for g in range(2):
            for d in range(1, NX):
                glob_copy(d, g).start()

    for d in (1, 3):
        pick(z, d, OWN_PLACE)
        give(d, OWN_PLACE, 1)
    pl.when(z == 0)(start_down)

    q_copies = []
    for d in range(1, NDP):
        q_copies.append(send(
            q_ref.at[:, pl.ds(pl.multiple_of(others[d] * WIDTH, WIDTH), WIDTH)], qbuf.at[own_rows],
            q_send.at[d], q_recv.at[d], at_p[d]))
        q_copies[-1].start()

    @pl.loop(1, NZ // 2)
    def _(k):
        slots = ((z + NZ - k) & (NZ - 1), (z + k) & (NZ - 1))
        for turn in range(2):
            for way in range(2):
                part = turn if way == 0 else 1 - turn
                z_part(slots[way], way, k, part).wait_recv()
                if part == way:
                    z_part(slots[way], way, k + 1, part).start()
                else:
                    pl.when(k < NZ // 2 - 1)(lambda: z_part(slots[way], way, k + 1, part).start())

        def share(d):
            for way in range(2):
                pick(slots[way], d, 2 * (k - 1) + way)
            give(d, 2 * (k - 1), 2, (0,))
            pl.when(k < LATE)(lambda: give(d, 2 * (k - 1), 2, (1,)))

        pl.when(k > NEAR)(lambda: share(2))
        share(1)
        share(3)

        @pl.when((z == 0) & (k == 1))
        def _():
            edge_copy(OWN - 1, 1).start()

        @pl.when((z == NZ - 1) & (k == 1))
        def _():
            edge_copy(0, NX - 1).start()

        pl.when((x != 0) & (hops == k - GLOB_LAG))(glob_pass)

        for hop in range(NEAR):
            @pl.when(k == OPP_AT[hop])
            def _():
                if hop == 0:
                    opp_first.wait_recv()
                for way in range(2):
                    if hop > 0:
                        opp_shard(way, hop - 1).wait_recv()
                    opp_shard(way, hop).start()

    far = (z + NZ // 2) & (NZ - 1)
    for way in range(2):
        z_part(far, way, NZ // 2, way).wait_recv()
    for d in (2, 1, 3):
        pick(far, d, FAR_PLACE)
        give(d, FAR_PLACE, 1, (0,))

    @pl.loop(LATE, NZ // 2)
    def _(k):
        for d in (2, 1, 3):
            give(d, 2 * (k - 1), 2, (1,))

    for d in (2, 1, 3):
        give(d, FAR_PLACE, 1, (1,))
    pl.when((x != 0) & (hops > NZ // 2 - 1 - GLOB_LAG))(glob_pass)

    for copy in q_copies:
        copy.wait()
    own_q.wait()

    def wait_given(part):
        for d in (1, 3, 2):
            count = NZ if d != 2 else NZ - 2 * NEAR - 1
            first = ((x - d) & (NX - 1)) * NZ
            landed = kv.at[pl.ds(RECV + first, count), 0] if part == 0 else given_v.at[pl.ds(first, count)]
            send(picked.at[d - 1, pl.ds(0, count), part], landed, x_send.at[part, d - 1], x_recv.at[part, d - 1],
                 at_x[d]).wait()

    if NEAR:
        for way in range(2):
            opp_shard(way, NEAR - 1).wait_recv()
    else:
        opp_first.wait_recv()

    @pl.when((z == 0) | (z == NZ - 1))
    def _():
        edge_copy(0, 1).wait()

    wait_given(0)

    every = []
    for i in range(KB):
        slots, given = [], [None] * 5
        if i == 0:
            slots.append(jnp.where(z == 0, EDGE, z * KB - 1))
        else:
            slots.append(z * KB + i - 1)
        slots.append(z * KB + i)
        if i == KB - 1:
            slots.append(jnp.where(z == NZ - 1, EDGE, z * KB + KB))
        else:
            slots.append(z * KB + i + 1)
        for g in range(2):
            slots.append(jnp.where(x == 0, g, GLOB + g))
        for e in range(5, LIST):
            block = list_ref[i, e]
            shard = (block * 21846) >> 16
            column, row, off = shard >> 4, shard & (NZ - 1), block - shard * KB
            ahead = ((row - z + NZ + NEAR) & (NZ - 1))
            ahead = (row - z) & (NZ - 1)
            place = jnp.where(ahead > NZ // 2, 2 * (NZ - 1 - ahead), 2 * ahead - 1)
            place = jnp.where(ahead == 0, OWN_PLACE, jnp.where(ahead == NZ // 2, FAR_PLACE, place))
            ahead = (ahead + NEAR) & (NZ - 1)
            near = (column == ((x + 2) & (NX - 1))) & (ahead <= 2 * NEAR)
            slot = jnp.where(near, OPP + ahead * KB + off, RECV + column * NZ + place)
            slots.append(jnp.where(column == x, row * KB + off, slot))
            given.append((jnp.where(near | (column == x), 0, 1), column * NZ + place))
        every.append((slots, given))
        for e in range(LIST):
            kcat[i, pl.ds(e * BLOCK, BLOCK)] = kv[slots[e], 0]

    factor = math.log2(math.e) / math.sqrt(HEAD_DIM)

    def head_cols(step):
        return [pl.ds(pl.multiple_of((step * PAIR + h) * HEAD_DIM, HEAD_DIM), HEAD_DIM) for h in range(PAIR)]

    @pl.loop(0, STEPS)
    def _(step):
        for i in range(KB):
            q = jnp.concatenate([qbuf[pl.ds(i * BLOCK, BLOCK), col] for col in head_cols(step)], axis=0)
            scores = lax.dot_general(q, kcat[i], (((1,), (1,)), ((), ())), preferred_element_type=jnp.float32)
            row_max = jnp.max(scores, axis=-1, keepdims=True)
            weights[step, i] = jnp.exp2((scores - row_max) * factor).astype(jnp.bfloat16)

    wait_given(1)
    for i in range(KB):
        for e in range(LIST):
            again = jnp.int32(0)
            for f in range(e):
                again = again | jnp.where(list_ref[i, e] == list_ref[i, f], 1, 0)
            keep = jnp.where(again == 1, 0.0, 1.0)
            mask = jnp.full((BLOCK, HEAD_DIM), keep, jnp.float32).astype(jnp.bfloat16)
            slots, given = every[i]
            rows = kv[slots[e], 1]
            if given[e] is not None:
                rows = jnp.where(given[e][0] == 1, given_v[given[e][1]], rows)
            vcat[i, pl.ds(e * BLOCK, BLOCK), pl.ds(0, HEAD_DIM)] = rows * mask
            vcat[i, pl.ds(e * BLOCK, BLOCK), pl.ds(HEAD_DIM, HEAD_DIM)] = mask

    def out_copy(d, step):
        return send(
            obuf.at[pl.ds(pl.multiple_of(others[d] * TOK, 16), TOK), pl.ds(pl.multiple_of(step * PAIR * HEAD_DIM, 256), PAIR * HEAD_DIM)],
            out_ref.at[:, pl.ds(pl.multiple_of(p * WIDTH + step * PAIR * HEAD_DIM, 256), PAIR * HEAD_DIM)],
            out_send, out_recv, at_p[d])

    @pl.loop(0, STEPS)
    def _(step):
        for i in range(KB):
            result = jnp.dot(weights[step, i], vcat[i], preferred_element_type=jnp.float32)
            result = (result[:, :HEAD_DIM] / result[:, HEAD_DIM:]).astype(jnp.bfloat16)
            for h, col in enumerate(head_cols(step)):
                obuf[pl.ds(i * BLOCK, BLOCK), col] = result[h * BLOCK:(h + 1) * BLOCK]
        for d in range(1, NDP):
            out_copy(d, step).start()

    own_out = pltpu.make_async_copy(
        obuf.at[pl.ds(pl.multiple_of(p * TOK, 16), TOK)],
        out_ref.at[:, pl.ds(pl.multiple_of(p * WIDTH, WIDTH), WIDTH)], own_out_sem)
    own_out.start()
    own_out.wait()

    for way in range(2):
        if NEAR:
            passed = blocks(0, NEAR * KB)
            send(passed, passed, opp_send.at[way], out_recv, at_z[way]).wait_send()
        sent = kv.at[pl.ds(0, (NZ - 1) * KB), 0]
        send(sent, sent, z_send.at[way], out_recv, at_z[way]).wait_send()
    opp_first.wait_send()

    @pl.when((x == 0) & (z == 0))
    def _():
        both = blocks(0, 2)
        for d in range(1, NX):
            send(both, both, glob_send.at[d], out_recv, at_x[d]).wait_send()

    def glob_sent(way):
        both = blocks(GLOB, 2)
        send(both, both, glob_send.at[way], out_recv, at_z[way]).wait_send()

    pl.when(up_on)(lambda: glob_sent(0))
    pl.when(down_on)(lambda: glob_sent(1))

    everything = out_ref.at[:, pl.ds(0, (NDP - 1) * WIDTH)]
    send(everything, everything, out_send, out_recv, at_p[1]).wait()


def shards(queries, keys, values, block_list):
    dma = pltpu.SemaphoreType.DMA
    bf16 = jnp.bfloat16
    hbm = pl.BlockSpec(memory_space=pl.ANY)
    return pl.pallas_call(
        kernel,
        out_shape=jax.ShapeDtypeStruct(queries.shape, queries.dtype),
        in_specs=[hbm] * 4,
        out_specs=hbm,
        scratch_shapes=[
            pltpu.VMEM((SLOTS, 2, BLOCK, HEAD_DIM), bf16),
            pltpu.VMEM((NX * NZ, BLOCK, HEAD_DIM), bf16),
            pltpu.VMEM((NX - 1, NZ, 2, BLOCK, HEAD_DIM), bf16),
            pltpu.VMEM((KB, LIST * BLOCK, HEAD_DIM), bf16),
            pltpu.VMEM((KB, LIST * BLOCK, 2 * HEAD_DIM), bf16),
            pltpu.VMEM((STEPS, KB, PAIR * BLOCK, LIST * BLOCK), bf16),
            pltpu.VMEM((SPAN, WIDTH), bf16),
            pltpu.VMEM((SPAN, WIDTH), bf16),
            pltpu.VMEM((NX, NZ, 128), jnp.int32),
            pltpu.VMEM((NX, NZ, 128), jnp.int32),
            pltpu.SMEM((NX, NZ, 128), jnp.int32),
            pltpu.SMEM((KB, LIST), jnp.int32),
            pltpu.SemaphoreType.REGULAR,
            dma, dma((2, KB)), dma, dma, dma((NX,)), dma((NX,)), dma, dma((NDP,)), dma((NDP,)),
            dma((2,)), dma((2, NZ // 2, 2)),
            dma((2, NX - 1)), dma((2, NX - 1)), dma((NX,)), dma((2,)), dma((3,)), dma((2, NEAR + 1)), dma, dma, dma, dma,
        ],
        compiler_params=pltpu.CompilerParams(
            collective_id=0, has_side_effects=True, vmem_limit_bytes=63 * 1024 * 1024
        ),
        name="gather_attend",
    )(block_list, queries, keys.reshape(KB, BLOCK, HEAD_DIM), values.reshape(KB, BLOCK, HEAD_DIM))


def solution(mesh):
    in_specs = (P(("ctx", "dp"), None), P("ctx", "dp"), P("ctx", "dp"), P("ctx", None))
    out_specs = P(("ctx", "dp"), None)
    return jax.shard_map(shards, mesh=mesh, in_specs=in_specs, out_specs=out_specs, check_vma=False)
```

```python
import math

import jax
import jax.numpy as jnp
from jax import lax
from jax.experimental import pallas as pl
from jax.experimental.pallas import tpu as pltpu
from jax.sharding import PartitionSpec as P

HEAD_DIM = 128
BLOCK = 128
LIST = 13
KB = 3
GROUP = 8
NX, NZ, NDP = 4, 16, 8
TOK = 48
WIDTH = GROUP * HEAD_DIM
SPAN = KB * BLOCK
OWN = NZ * KB
RECV = OWN
GLOB = RECV + NX * NZ
EDGE = GLOB + 2
OPP_AT = (5, 7)
OWN_PLACE, FAR_PLACE = NZ - 2, NZ - 1
GLOB_LAG = 3
LATE = 7
NEAR = 2
OPP = EDGE + 1
SLOTS = OPP + (2 * NEAR + 1) * KB
PAIR = 2
STEPS = GROUP // PAIR
MESH = pl.DeviceIdType.MESH


def kernel(lists, q_ref, k_ref, v_ref, out_ref, kv, given_v, picked, kcat, vcat, weights, qbuf, obuf, ask, asked, asked_s, list_ref, lower_in,
           list_sem, load_sem, own_q_sem, own_out_sem, ask_send, ask_recv, asked_sem, q_send, q_recv, z_send, z_recv, x_send, x_recv,
           glob_send, glob_recv, opp_send, opp_recv, edge_send, edge_recv, out_send, out_recv):
    c = lax.axis_index("ctx")
    p = lax.axis_index("dp")
    x = c // NZ
    z = c & (NZ - 1)
    at_x = [{"ctx": ((x + d) & (NX - 1)) * NZ + z, "dp": p} for d in range(NX)]
    at_z = [{"ctx": x * NZ + ((z + d) & (NZ - 1)), "dp": p} for d in (1, NZ - 1)]
    others = [(p + d) & (NDP - 1) for d in range(NDP)]
    at_p = [{"ctx": c, "dp": t} for t in others]

    def send(src, dst, ssem, rsem, dev):
        return pltpu.make_async_remote_copy(
            src_ref=src, dst_ref=dst, send_sem=ssem, recv_sem=rsem, device_id=dev, device_id_type=MESH
        )

    def blocks(slot, count):
        return kv.at[pl.ds(slot, count)]

    list_copy = pltpu.make_async_copy(lists, list_ref, list_sem)
    list_copy.start()
    barrier = pltpu.get_barrier_semaphore()
    for dev in at_x[1:] + at_z[1:] + at_p[1:]:
        pl.semaphore_signal(barrier, inc=1, device_id=dev, device_id_type=MESH)

    loads = []
    for b in range(KB):
        loads.append(pltpu.make_async_copy(k_ref.at[b], kv.at[z * KB + b, 0], load_sem.at[0, b]))
        loads.append(pltpu.make_async_copy(v_ref.at[b], kv.at[z * KB + b, 1], load_sem.at[1, b]))
    for copy in loads:
        copy.start()
    own_rows = pl.ds(pl.multiple_of(p * TOK, 16), TOK)
    own_q = pltpu.make_async_copy(
        q_ref.at[:, pl.ds(pl.multiple_of(p * WIDTH, WIDTH), WIDTH)], qbuf.at[own_rows], own_q_sem)
    own_q.start()

    list_copy.wait()
    rows = lax.broadcasted_iota(jnp.int32, (NX * NZ, 128), 0) * KB
    wanted = jnp.zeros((NX * NZ, 128), jnp.int32)
    for i in range(KB):
        for e in range(5, LIST):
            off = list_ref[i, e] - rows
            wanted = wanted + jnp.where(off == 1, 1, 0) + jnp.where(off == 2, 2, 0)
    ask[...] = wanted.reshape(NX, NZ, 128)

    for copy in loads:
        copy.wait()
    pl.semaphore_wait(barrier, NX - 1 + 1 + NDP - 1)
    pl.semaphore_signal(lower_in, inc=1, device_id=at_z[0], device_id_type=MESH)

    def z_part(slot, way, k, part):
        half = kv.at[pl.ds(KB * slot, KB), part]
        return send(half, half, z_send.at[way], z_recv.at[way, k - 1, part], at_z[way])

    for part in range(2):
        z_part(z, 0, 1, part).start()

    asks = []
    for d in range(1, NX):
        asks.append(send(ask.at[(x + d) & (NX - 1)], asked.at[d], ask_send.at[d], ask_recv.at[d], at_x[d]))
        asks[-1].start()

    def opp_shard(way, hop):
        row, step = (-hop, -1) if way == 0 else (hop, 1)
        return send(blocks(OPP + (row + NEAR) * KB, KB), blocks(OPP + (row + step + NEAR) * KB, KB),
                    opp_send.at[way], opp_recv.at[way, hop + 1], at_z[way])

    opp_first = send(blocks(z * KB, KB), blocks(OPP + NEAR * KB, KB), opp_send.at[2], opp_recv.at[0, 0], at_x[2])
    opp_first.start()

    def start_down():
        pl.semaphore_wait(lower_in, 1)
        for part in (1, 0):
            z_part(z, 1, 1, part).start()

    pl.when(z != 0)(start_down)

    for copy in asks:
        copy.wait()
    to_scalars = pltpu.make_async_copy(asked, asked_s, asked_sem)
    to_scalars.start()

    def glob_copy(d, g):
        return send(blocks(g, 1), blocks(GLOB + g, 1), glob_send.at[d], glob_recv.at[g], at_x[d])

    def glob_on(way, g):
        one = blocks(GLOB + g, 1)
        return send(one, one, glob_send.at[way], glob_recv.at[g], at_z[way])

    hops = jnp.where(z > NZ // 2, NZ - z, z)
    up_on = (x != 0) & (z < NZ // 2)
    down_on = (x != 0) & ((z == 0) | (z > NZ // 2 + 1))

    def glob_pass():
        for g in range(2):
            glob_on(0, g).wait_recv()
            pl.when(up_on)(lambda: glob_on(0, g).start())
            pl.when(down_on)(lambda: glob_on(1, g).start())

    def edge_copy(slot, d):
        return send(blocks(slot, 1), blocks(EDGE, 1), edge_send, edge_recv, at_x[d])

    def pick(slot, d, place):
        first, second, third = (kv[slot * KB + b] for b in range(KB))
        off = asked_s[NX - d, slot, 0]
        picked[d - 1, place] = jnp.where(off == 1, second, jnp.where(off == 2, third, first))

    def give(d, place, count, parts=(0, 1)):
        for part in parts:
            if part == 0:
                target = kv.at[pl.ds(RECV + x * NZ + place, count), 0]
            else:
                target = given_v.at[pl.ds(x * NZ + place, count)]
            send(picked.at[d - 1, pl.ds(place, count), part], target,
                 x_send.at[part, d - 1], x_recv.at[part, d - 1], at_x[d]).start()

    to_scalars.wait()

    @pl.when((x == 0) & (z == 0))
    def _():
        for g in range(2):
            for d in range(1, NX):
                glob_copy(d, g).start()

    for d in (1, 3):
        pick(z, d, OWN_PLACE)
        give(d, OWN_PLACE, 1)
    pl.when(z == 0)(start_down)

    q_copies = []
    for d in range(1, NDP):
        q_copies.append(send(
            q_ref.at[:, pl.ds(pl.multiple_of(others[d] * WIDTH, WIDTH), WIDTH)], qbuf.at[own_rows],
            q_send.at[d], q_recv.at[d], at_p[d]))
        q_copies[-1].start()

    @pl.loop(1, NZ // 2)
    def _(k):
        slots = ((z + NZ - k) & (NZ - 1), (z + k) & (NZ - 1))
        for turn in range(2):
            for way in range(2):
                part = turn if way == 0 else 1 - turn
                z_part(slots[way], way, k, part).wait_recv()
                if part == way:
                    z_part(slots[way], way, k + 1, part).start()
                else:
                    pl.when(k < NZ // 2 - 1)(lambda: z_part(slots[way], way, k + 1, part).start())

        def share(d):
            for way in range(2):
                pick(slots[way], d, 2 * (k - 1) + way)
            give(d, 2 * (k - 1), 2, (0,))
            pl.when(k < LATE)(lambda: give(d, 2 * (k - 1), 2, (1,)))

        pl.when(k > NEAR)(lambda: share(2))
        share(1)
        share(3)

        @pl.when((z == 0) & (k == 1))
        def _():
            edge_copy(OWN - 1, 1).start()

        @pl.when((z == NZ - 1) & (k == 1))
        def _():
            edge_copy(0, NX - 1).start()

        pl.when((x != 0) & (hops == k - GLOB_LAG))(glob_pass)

        for hop in range(NEAR):
            @pl.when(k == OPP_AT[hop])
            def _():
                if hop == 0:
                    opp_first.wait_recv()
                for way in range(2):
                    if hop > 0:
                        opp_shard(way, hop - 1).wait_recv()
                    opp_shard(way, hop).start()

    far = (z + NZ // 2) & (NZ - 1)
    for way in range(2):
        z_part(far, way, NZ // 2, way).wait_recv()
    for d in (2, 1, 3):
        pick(far, d, FAR_PLACE)
        give(d, FAR_PLACE, 1, (0,))

    @pl.loop(LATE, NZ // 2)
    def _(k):
        for d in (2, 1, 3):
            give(d, 2 * (k - 1), 2, (1,))

    for d in (2, 1, 3):
        give(d, FAR_PLACE, 1, (1,))
    pl.when((x != 0) & (hops > NZ // 2 - 1 - GLOB_LAG))(glob_pass)

    for copy in q_copies:
        copy.wait()
    own_q.wait()

    def wait_given(part):
        for d in (1, 3, 2):
            count = NZ if d != 2 else NZ - 2 * NEAR - 1
            first = ((x - d) & (NX - 1)) * NZ
            landed = kv.at[pl.ds(RECV + first, count), 0] if part == 0 else given_v.at[pl.ds(first, count)]
            send(picked.at[d - 1, pl.ds(0, count), part], landed, x_send.at[part, d - 1], x_recv.at[part, d - 1],
                 at_x[d]).wait()

    if NEAR:
        for way in range(2):
            opp_shard(way, NEAR - 1).wait_recv()
    else:
        opp_first.wait_recv()

    @pl.when((z == 0) | (z == NZ - 1))
    def _():
        edge_copy(0, 1).wait()

    wait_given(0)

    every = []

    def fill(keep):
        return jnp.full((BLOCK, HEAD_DIM), keep, jnp.float32).astype(jnp.bfloat16)

    for i in range(KB):
        slots, given = [], [None] * 5
        if i == 0:
            slots.append(jnp.where(z == 0, EDGE, z * KB - 1))
        else:
            slots.append(z * KB + i - 1)
        slots.append(z * KB + i)
        if i == KB - 1:
            slots.append(jnp.where(z == NZ - 1, EDGE, z * KB + KB))
        else:
            slots.append(z * KB + i + 1)
        for g in range(2):
            slots.append(jnp.where(x == 0, g, GLOB + g))
        for e in range(5, LIST):
            block = list_ref[i, e]
            shard = (block * 21846) >> 16
            column, row, off = shard >> 4, shard & (NZ - 1), block - shard * KB
            ahead = ((row - z + NZ + NEAR) & (NZ - 1))
            ahead = (row - z) & (NZ - 1)
            place = jnp.where(ahead > NZ // 2, 2 * (NZ - 1 - ahead), 2 * ahead - 1)
            place = jnp.where(ahead == 0, OWN_PLACE, jnp.where(ahead == NZ // 2, FAR_PLACE, place))
            ahead = (ahead + NEAR) & (NZ - 1)
            near = (column == ((x + 2) & (NX - 1))) & (ahead <= 2 * NEAR)
            slot = jnp.where(near, OPP + ahead * KB + off, RECV + column * NZ + place)
            slots.append(jnp.where(column == x, row * KB + off, slot))
            given.append((jnp.where(near | (column == x), 0, 1), column * NZ + place))
        keeps = []
        for e in range(LIST):
            again = jnp.int32(0)
            for f in range(e):
                again = again | jnp.where(list_ref[i, e] == list_ref[i, f], 1, 0)
            keeps.append(jnp.where(again == 1, 0.0, 1.0))
            vcat[i, pl.ds(e * BLOCK, BLOCK), pl.ds(HEAD_DIM, HEAD_DIM)] = fill(keeps[e])
        for e in range(5):
            vcat[i, pl.ds(e * BLOCK, BLOCK), pl.ds(0, HEAD_DIM)] = kv[slots[e], 1] * fill(keeps[e])
        every.append((slots, given, keeps))
        for e in range(LIST):
            kcat[i, pl.ds(e * BLOCK, BLOCK)] = kv[slots[e], 0]

    factor = math.log2(math.e) / math.sqrt(HEAD_DIM)

    def head_cols(step):
        return [pl.ds(pl.multiple_of((step * PAIR + h) * HEAD_DIM, HEAD_DIM), HEAD_DIM) for h in range(PAIR)]

    @pl.loop(0, STEPS)
    def _(step):
        for i in range(KB):
            q = jnp.concatenate([qbuf[pl.ds(i * BLOCK, BLOCK), col] for col in head_cols(step)], axis=0)
            scores = lax.dot_general(q, kcat[i], (((1,), (1,)), ((), ())), preferred_element_type=jnp.float32)
            row_max = jnp.max(scores, axis=-1, keepdims=True)
            weights[step, i] = jnp.exp2((scores - row_max) * factor).astype(jnp.bfloat16)

    wait_given(1)
    for i in range(KB):
        slots, given, keeps = every[i]
        for e in range(5, LIST):
            rows = jnp.where(given[e][0] == 1, given_v[given[e][1]], kv[slots[e], 1])
            vcat[i, pl.ds(e * BLOCK, BLOCK), pl.ds(0, HEAD_DIM)] = rows * fill(keeps[e])

    def out_copy(d, step):
        return send(
            obuf.at[pl.ds(pl.multiple_of(others[d] * TOK, 16), TOK), pl.ds(pl.multiple_of(step * PAIR * HEAD_DIM, 256), PAIR * HEAD_DIM)],
            out_ref.at[:, pl.ds(pl.multiple_of(p * WIDTH + step * PAIR * HEAD_DIM, 256), PAIR * HEAD_DIM)],
            out_send, out_recv, at_p[d])

    @pl.loop(0, STEPS)
    def _(step):
        for i in range(KB):
            result = jnp.dot(weights[step, i], vcat[i], preferred_element_type=jnp.float32)
            result = (result[:, :HEAD_DIM] / result[:, HEAD_DIM:]).astype(jnp.bfloat16)
            for h, col in enumerate(head_cols(step)):
                obuf[pl.ds(i * BLOCK, BLOCK), col] = result[h * BLOCK:(h + 1) * BLOCK]
        for d in range(1, NDP):
            out_copy(d, step).start()

    own_out = pltpu.make_async_copy(
        obuf.at[pl.ds(pl.multiple_of(p * TOK, 16), TOK)],
        out_ref.at[:, pl.ds(pl.multiple_of(p * WIDTH, WIDTH), WIDTH)], own_out_sem)
    own_out.start()
    own_out.wait()

    for way in range(2):
        if NEAR:
            passed = blocks(0, NEAR * KB)
            send(passed, passed, opp_send.at[way], out_recv, at_z[way]).wait_send()
        sent = kv.at[pl.ds(0, (NZ - 1) * KB), 0]
        send(sent, sent, z_send.at[way], out_recv, at_z[way]).wait_send()
    opp_first.wait_send()

    @pl.when((x == 0) & (z == 0))
    def _():
        both = blocks(0, 2)
        for d in range(1, NX):
            send(both, both, glob_send.at[d], out_recv, at_x[d]).wait_send()

    def glob_sent(way):
        both = blocks(GLOB, 2)
        send(both, both, glob_send.at[way], out_recv, at_z[way]).wait_send()

    pl.when(up_on)(lambda: glob_sent(0))
    pl.when(down_on)(lambda: glob_sent(1))

    everything = out_ref.at[:, pl.ds(0, (NDP - 1) * WIDTH)]
    send(everything, everything, out_send, out_recv, at_p[1]).wait()


def shards(queries, keys, values, block_list):
    dma = pltpu.SemaphoreType.DMA
    bf16 = jnp.bfloat16
    hbm = pl.BlockSpec(memory_space=pl.ANY)
    return pl.pallas_call(
        kernel,
        out_shape=jax.ShapeDtypeStruct(queries.shape, queries.dtype),
        in_specs=[hbm] * 4,
        out_specs=hbm,
        scratch_shapes=[
            pltpu.VMEM((SLOTS, 2, BLOCK, HEAD_DIM), bf16),
            pltpu.VMEM((NX * NZ, BLOCK, HEAD_DIM), bf16),
            pltpu.VMEM((NX - 1, NZ, 2, BLOCK, HEAD_DIM), bf16),
            pltpu.VMEM((KB, LIST * BLOCK, HEAD_DIM), bf16),
            pltpu.VMEM((KB, LIST * BLOCK, 2 * HEAD_DIM), bf16),
            pltpu.VMEM((STEPS, KB, PAIR * BLOCK, LIST * BLOCK), bf16),
            pltpu.VMEM((SPAN, WIDTH), bf16),
            pltpu.VMEM((SPAN, WIDTH), bf16),
            pltpu.VMEM((NX, NZ, 128), jnp.int32),
            pltpu.VMEM((NX, NZ, 128), jnp.int32),
            pltpu.SMEM((NX, NZ, 128), jnp.int32),
            pltpu.SMEM((KB, LIST), jnp.int32),
            pltpu.SemaphoreType.REGULAR,
            dma, dma((2, KB)), dma, dma, dma((NX,)), dma((NX,)), dma, dma((NDP,)), dma((NDP,)),
            dma((2,)), dma((2, NZ // 2, 2)),
            dma((2, NX - 1)), dma((2, NX - 1)), dma((NX,)), dma((2,)), dma((3,)), dma((2, NEAR + 1)), dma, dma, dma, dma,
        ],
        compiler_params=pltpu.CompilerParams(
            collective_id=0, has_side_effects=True, vmem_limit_bytes=63 * 1024 * 1024
        ),
        name="gather_attend",
    )(block_list, queries, keys.reshape(KB, BLOCK, HEAD_DIM), values.reshape(KB, BLOCK, HEAD_DIM))


def solution(mesh):
    in_specs = (P(("ctx", "dp"), None), P("ctx", "dp"), P("ctx", "dp"), P("ctx", None))
    out_specs = P(("ctx", "dp"), None)
    return jax.shard_map(shards, mesh=mesh, in_specs=in_specs, out_specs=out_specs, check_vma=False)
```
